32 devices in a mesh: dp: 2 (over x), cp: 16 (over z, y, core).
Axes of the slice: x: 2, y: 2, z: 4, core: 2. Of those that a mesh axis runs over, the one named last changes fastest.
Arguments:
- tokens: bfloat16 [2, 2, 1024, 1536], P(None, 'dp', 'cp'), may hold values from -6 to 6
- cotangent: bfloat16 [2, 2, 1024, 1536], P(None, 'dp', 'cp'), may hold values from -6 to 6
- segments: int32 [2, 2, 1024], P(None, 'dp'), may hold values from 0 to 3, never falling along the last dimension, each value on 1 to 800 neighbouring positions
- span_order: int32 [32], replicated, may hold values from 0 to 31, as said below
- pre_gain: bfloat16 [1536], P(('dp', 'cp')), may hold values from 0.5 to 1.5
- query_proj: bfloat16 [1536, 1536], P(('dp', 'cp')), may hold values from -0.15625 to 0.15625
- key_proj: bfloat16 [1536, 512], P(('dp', 'cp')), may hold values from -0.15625 to 0.15625
- value_proj: bfloat16 [1536, 512], P(('dp', 'cp')), may hold values from -0.15625 to 0.15625
- head_gain: bfloat16 [128], P(('dp', 'cp')), may hold values from 0.5 to 1.5
- out_proj: bfloat16 [1536, 1536], P(('dp', 'cp')), may hold values from -0.625 to 0.625
- mid_gain: bfloat16 [1536], P(('dp', 'cp')), may hold values from 0.5 to 1.5
- gate_proj: bfloat16 [1536, 6912], P(('dp', 'cp')), may hold values from -0.15625 to 0.15625
- up_proj: bfloat16 [1536, 6912], P(('dp', 'cp')), may hold values from -0.15625 to 0.15625
- down_proj: bfloat16 [6912, 1536], P(('dp', 'cp')), may hold values from -0.078125 to 0.078125
Outputs:
- block_out: bfloat16 [2, 2, 1024, 1536], P(None, 'dp', 'cp')
- grad_tokens: float32 [2, 2, 1024, 1536], P(None, 'dp', 'cp')
- grad_pre_gain: float32 [1536], P(('dp', 'cp'))
- grad_query: float32 [1536, 1536], P(('dp', 'cp'))
- grad_key: float32 [1536, 512], P(('dp', 'cp'))
- grad_value: float32 [1536, 512], P(('dp', 'cp'))
- grad_head_gain: float32 [128], P(('dp', 'cp'))
- grad_output: float32 [1536, 1536], P(('dp', 'cp'))
- grad_mid_gain: float32 [1536], P(('dp', 'cp'))
- grad_gate: float32 [1536, 6912], P(('dp', 'cp'))
- grad_upward: float32 [1536, 6912], P(('dp', 'cp'))
- grad_down: float32 [6912, 1536], P(('dp', 'cp'))
The draws below stay inside these ranges and needn't reach their ends.
Inputs may be any that keep to these rules, and one draw needn't show every extreme that they name: `segments`: document numbers never fall along a sequence; each of the 4 documents has 1 to 800 tokens, and one has exactly 800. `span_order`: mirrored pairs: each span number appears once, and stored spans 2j and 2j+1 hold two span numbers that add up to 31.
All inputs are finite; a program needn't handle non-finite values.
Results may differ from the reference program's by a relative error of at most 0.035.
Values may be sent and summed in bfloat16 or wider, within the bound.
A program may use at most 448 MiB of HBM per device.

```python
import math
import jax
import jax.numpy as jnp
import numpy as np
from jax import lax

D = 1536
HEADS = 24
KVH = 8
HD = 64
FF = 6912
MICRO = 2
MAXDOC = 800
LEN = 1024
SEQS = 2
DOCS = 4
SPANS = 32
QW = 1536
KW = 512


def draw_span_order(key, part):
    key = jax.random.fold_in(key, 5)
    pairs = SPANS // 2
    chosen = jax.random.permutation(key, jnp.arange(pairs, dtype=jnp.int32))
    mirrored = SPANS - 1 - chosen
    return jnp.stack([chosen, mirrored], axis=1).reshape(SPANS).astype(jnp.int32)


def block_scale(stream_key, shape, pieces, smallest, largest):
    level, own = 1.0, jax.random.fold_in(stream_key, 6)
    for axis_at, blocks in pieces:
        steps = jnp.exp(jax.random.uniform(jax.random.fold_in(own, axis_at), (blocks,), jnp.float32, smallest / len(pieces), largest / len(pieces)))
        level = level * jnp.repeat(steps, shape[axis_at] // blocks).reshape([-1 if axis == axis_at else 1 for axis in range(len(shape))])
    return level


def length_profile(number_of, total, bound, slope):
    portions = [(1 << 20) // math.isqrt(rank ** slope) + 1 for rank in range(2, number_of + 1)]
    surplus, given = total - bound - (number_of - 1), [1] * (number_of - 1)
    while surplus > 0:
        free = [i for i in range(number_of - 1) if given[i] < bound]
        mass, remaining = sum([portions[i] for i in free]), surplus
        for i in free:
            addition = min(bound - given[i], max(1, remaining * portions[i] // mass), surplus)
            given[i] = given[i] + addition
            surplus = surplus - addition
    return np.array([bound] + given)


def uneven_parts(stream_key, count, total, bound, lean):
    if count == 2:
        one = jax.random.randint(stream_key, (), max(1, total - bound), min(bound, total - 1) + 1)
        return jnp.stack([one, total - one])
    tallies = jnp.asarray(length_profile(count, total, bound, lean), jnp.int32)
    twos = (count - 1) // 2
    giver, receiver = tallies[1:1 + 2 * twos:2], tallies[2:2 + 2 * twos:2]
    room = jnp.minimum(giver - 1, bound - receiver)
    moved = jax.random.randint(jax.random.fold_in(stream_key, 1), (twos,), 0, 1 << 20) % (room + 1)
    tallies = tallies.at[1:1 + 2 * twos:2].set(giver - moved).at[2:2 + 2 * twos:2].set(receiver + moved)
    return tallies[jax.random.permutation(jax.random.fold_in(stream_key, 2), count)]


def centred(stream_key, extent, scale, bound, cuts=(), kind=jnp.bfloat16):
    gain = block_scale(stream_key, extent, cuts, -0.22, 0.18) if cuts else 1.0
    drawn = jax.random.normal(stream_key, extent, jnp.float32) * scale * gain
    return jnp.minimum(jnp.maximum(drawn, -bound), bound).astype(kind)


def setup_inputs(seed: int = 0) -> dict:
    key_of = jax.random.split(jax.random.key(seed), 15)
    return {
        "tokens": centred(key_of[0], (MICRO, SEQS, LEN, D), 1.0, 6.0, ((1, 2), (2, 16))),
        "cotangent": centred(key_of[1], (MICRO, SEQS, LEN, D), 1.0, 6.0, ((1, 2), (2, 16))),
        "segments": jax.vmap(lambda own: jnp.searchsorted(jnp.cumsum(uneven_parts(own, DOCS, LEN, MAXDOC, 1)), jnp.arange(LEN), side="right"))(jax.random.split(key_of[2], MICRO * SEQS)).reshape((MICRO, SEQS, LEN)).astype(jnp.int32),
        "span_order": draw_span_order(jax.random.fold_in(key_of[14], 71), 0),
        "pre_gain": jnp.clip(1.0 + 0.1 * jax.random.normal(key_of[4], (D,), jnp.float32), 0.5, 1.5).astype(jnp.bfloat16),
        "query_proj": centred(key_of[5], (D, QW), D ** -0.5, 0.15625, ((0, 32),)),
        "key_proj": centred(key_of[6], (D, KW), D ** -0.5, 0.15625, ((0, 32),)),
        "value_proj": centred(key_of[7], (D, KW), D ** -0.5, 0.15625, ((0, 32),)),
        "head_gain": jnp.clip(1.0 + 0.1 * jax.random.normal(key_of[8], (2 * HD,), jnp.float32), 0.5, 1.5).astype(jnp.bfloat16),
        "out_proj": centred(key_of[9], (QW, D), (QW // 16) ** -0.5, 0.625, ((0, 32),)),
        "mid_gain": jnp.clip(1.0 + 0.1 * jax.random.normal(key_of[10], (D,), jnp.float32), 0.5, 1.5).astype(jnp.bfloat16),
        "gate_proj": centred(key_of[11], (D, FF), D ** -0.5, 0.15625, ((0, 32),)),
        "up_proj": centred(key_of[12], (D, FF), D ** -0.5, 0.15625, ((0, 32),)),
        "down_proj": centred(key_of[13], (FF, D), FF ** -0.5, 0.078125, ((0, 32),)),
    }


@jax.custom_vjp
def low(v):
    return lax.optimization_barrier(v.astype(jnp.bfloat16)).astype(jnp.float32)

@jax.custom_vjp
def low_back(v):
    return v

def low_keep(v):
    return (low(v), None)

def low_pass(kept, grad):
    return (grad,)

def back_keep(v):
    return (v, None)

def back_low(kept, grad):
    return (low(grad),)
low.defvjp(low_keep, low_pass)
low_back.defvjp(back_keep, back_low)
highest = lax.Precision.HIGHEST
epsilon = 1e-05
theta_base = 1000000.0

def rms_norm(values, gain_vec):
    return values * lax.rsqrt(lax.optimization_barrier(jnp.mean(values * values, axis=-1, keepdims=True)) + epsilon) * gain_vec

def rotate(values, angles):
    half_width = values.shape[-1] // 2
    first_half = values[..., :half_width]
    second_half = values[..., half_width:]
    cosine = jnp.cos(angles)
    sine_part = jnp.sin(angles)
    return jnp.concatenate([first_half * cosine - second_half * sine_part, second_half * cosine + first_half * sine_part], axis=-1)

def rope_angles(doc_places, head_width):
    frequency = theta_base ** (-jnp.arange(0, head_width, 2).astype(jnp.float32) / head_width)
    return doc_places.astype(jnp.float32)[..., None] * frequency

def stored_places(span_order, length):
    span_rows = length // span_order.shape[0]
    stored = jnp.arange(length, dtype=jnp.int32)
    return span_order[stored // span_rows] * span_rows + stored % span_rows

def document_places(doc_ids):
    length = doc_ids.shape[-1]
    indices = jnp.broadcast_to(jnp.arange(length, dtype=jnp.int32), doc_ids.shape)
    changed = jnp.concatenate([jnp.ones(doc_ids.shape[:-1] + (1,), jnp.bool_), doc_ids[..., 1:] != doc_ids[..., :-1]], axis=-1)
    starts = lax.cummax(jnp.where(changed, indices, 0), axis=doc_ids.ndim - 1)
    return indices - starts

def layer(inputs, weights, doc_ids, places, angles):
    pre_gain, query_proj, key_proj, value_proj, head_gain, out_proj, mid_gain, gate_proj, up_proj, down_proj = weights
    length = inputs.shape[0]
    group_size = HEADS // KVH
    normed = low(rms_norm(inputs, pre_gain))
    query_raw = low_back(jnp.dot(normed, query_proj, precision=highest)).reshape(length, HEADS, HD)
    key_raw = low_back(jnp.dot(normed, key_proj, precision=highest)).reshape(length, KVH, HD)
    values = low(low_back(jnp.dot(normed, value_proj, precision=highest))).reshape(length, KVH, HD)
    queries = low(rotate(rms_norm(query_raw, head_gain[:HD]), angles[:, None, :]))
    key_rows = low(rotate(rms_norm(key_raw, head_gain[HD:]), angles[:, None, :]))
    block_rows = min(512, length)
    grouped = queries.reshape(length // block_rows, block_rows, KVH, group_size, HD)

    def attend(block_args):
        query_block, doc_block, place_block = block_args
        scores = low_back(HD ** (-0.5) * jnp.einsum('qhgd,khd->hgqk', query_block, key_rows, precision=highest))
        allowed = (doc_block[:, None] == doc_ids[None, :]) & (places[None, :] <= place_block[:, None])
        masked = jnp.where(allowed, scores, -1e+30)
        unscaled = jnp.where(allowed, jnp.exp(masked - lax.optimization_barrier(jnp.max(masked, axis=-1, keepdims=True))), 0.0)
        probability = low(unscaled / lax.optimization_barrier(jnp.sum(unscaled, axis=-1, keepdims=True)))
        return jnp.einsum('hgqk,khd->qhgd', probability, values, precision=highest)
    attended = lax.map(jax.checkpoint(attend), (grouped, doc_ids.reshape(-1, block_rows), places.reshape(-1, block_rows)))
    attended = low(low_back(attended.reshape(length, HEADS * HD)))
    middle = inputs + low_back(jnp.dot(attended, out_proj, precision=highest))
    normed_mid = low(rms_norm(middle, mid_gain))
    gate_pre = low_back(jnp.dot(normed_mid, gate_proj, precision=highest))
    upward = low_back(jnp.dot(normed_mid, up_proj, precision=highest))
    hidden_act = low(jax.nn.silu(gate_pre) * upward)
    return middle + jnp.dot(hidden_act, down_proj, precision=highest)

def reference(tokens, cotangent, segments, span_order, pre_gain, query_proj, key_proj, value_proj, head_gain, out_proj, mid_gain, gate_proj, up_proj, down_proj):
    length = tokens.shape[2]
    model_width = tokens.shape[3]
    places = stored_places(span_order, length)
    weights = tuple((argument.astype(jnp.float32) for argument in (pre_gain, query_proj, key_proj, value_proj, head_gain, out_proj, mid_gain, gate_proj, up_proj, down_proj)))
    flat_tokens = tokens.reshape(-1, length, model_width)
    flat_cot = cotangent.reshape(-1, length, model_width)
    flat_docs = segments.reshape(-1, length)

    def one_sequence(totals, entry):
        seq_tokens, seq_cot, seq_docs = entry
        doc_ids = seq_docs[places]
        angles = rope_angles(document_places(seq_docs)[places], HD)

        def forward(inputs, params):
            return layer(inputs, params, doc_ids, places, angles)
        result, pullback = jax.vjp(forward, seq_tokens.astype(jnp.float32), weights)
        grad_inputs, grad_params = pullback(seq_cot.astype(jnp.float32))
        totals = tuple((running + fresh for running, fresh in zip(totals, grad_params)))
        return (totals, (result.astype(jnp.bfloat16), grad_inputs))
    initial = tuple((jnp.zeros(argument.shape, jnp.float32) for argument in weights))
    totals, (block_out, grad_tokens) = lax.scan(one_sequence, initial, (flat_tokens, flat_cot, flat_docs))
    return (block_out.reshape(tokens.shape), grad_tokens.reshape(tokens.shape), totals[0], totals[1], totals[2], totals[3], totals[4], totals[5], totals[6], totals[7], totals[8], totals[9])
```

```python
import jax
import jax.numpy as jnp
from jax import lax
from jax.sharding import PartitionSpec as P

HD = 64
EPS = 1e-05
THETA = 1000000.0
BF = jnp.bfloat16
F32 = jnp.float32


def rms_norm(values, gain):
    return values * lax.rsqrt(jnp.mean(values * values, axis=-1, keepdims=True) + EPS) * gain


def rotate(values, angles):
    half = values.shape[-1] // 2
    a, b = values[..., :half], values[..., half:]
    cosine, sine = jnp.cos(angles), jnp.sin(angles)
    return jnp.concatenate([a * cosine - b * sine, b * cosine + a * sine], axis=-1)


def document_places(doc_ids):
    length = doc_ids.shape[-1]
    indices = jnp.arange(length, dtype=jnp.int32)
    changed = jnp.concatenate([jnp.ones((1,), jnp.bool_), doc_ids[1:] != doc_ids[:-1]])
    starts = lax.cummax(jnp.where(changed, indices, 0), axis=0)
    return indices - starts


def dot(a, b):
    return jnp.dot(a, b, preferred_element_type=F32)


def dot_nt(a, b):
    return lax.dot_general(a, b, (((1,), (1,)), ((), ())), preferred_element_type=F32)


def dot_tn(a, b):
    return lax.dot_general(a, b, (((0,), (0,)), ((), ())), preferred_element_type=F32)


def attention_fwd(q, k, v, allowed):
    scores = jnp.einsum("gqd,kd->gqk", q, k, preferred_element_type=F32) * HD**-0.5
    masked = jnp.where(allowed[None], scores, -1e30)
    top = jnp.max(masked, axis=-1, keepdims=True)
    unscaled = jnp.exp(masked - top)
    total = jnp.sum(unscaled, axis=-1, keepdims=True)
    attended = jnp.einsum("gqk,kd->gqd", unscaled.astype(BF), v, preferred_element_type=F32) / total
    return attended, top + jnp.log(total)


def attention_bwd(q, k, v, allowed, log_total, delta, gm):
    scores = jnp.einsum("gqd,kd->gqk", q, k, preferred_element_type=F32) * HD**-0.5
    prob = jnp.exp(jnp.where(allowed[None], scores, -1e30) - log_total)
    grad_v = jnp.einsum("gqk,gqd->kd", prob.astype(BF), gm, preferred_element_type=F32)
    grad_prob = jnp.einsum("gqd,kd->gqk", gm, v, preferred_element_type=F32)
    gs = (prob * (grad_prob - delta)).astype(BF)
    grad_q = jnp.einsum("gqk,kd->gqd", gs, k, preferred_element_type=F32) * HD**-0.5
    grad_k = jnp.einsum("gqk,gqd->kd", gs, q, preferred_element_type=F32) * HD**-0.5
    return grad_q, grad_k, grad_v


def head_norm(raw, gain, angles):
    return rotate(rms_norm(raw, gain), angles)


def local(tokens, cotangent, segments, span_order, pre_gain, query_proj, key_proj, value_proj,
          head_gain, out_proj, mid_gain, gate_proj, up_proj, down_proj):
    micros, seqs, rows, width = tokens.shape
    both = ("dp", "cp")
    cp = lax.axis_size("cp")
    dp = lax.axis_size("dp")
    me = lax.axis_index("cp")
    length = rows * cp
    kvh = key_proj.shape[1] // HD
    group = query_proj.shape[1] // key_proj.shape[1]
    qcols = group * HD
    wrows = gate_proj.shape[0]
    ffs = down_proj.shape[0]
    own = micros * seqs * rows
    my_seq, my_head = me // kvh, me % kvh

    packed = jnp.concatenate([pre_gain, mid_gain, head_gain])
    gains = lax.all_gather(packed, both, axis=0, tiled=False).astype(F32)
    pre_full = gains[:, :wrows].reshape(-1)
    mid_full = gains[:, wrows : 2 * wrows].reshape(-1)
    head_full = gains[:, 2 * wrows :].reshape(-1)

    def shuffle(weight, parts):
        pieces = weight.reshape(wrows, parts, -1).transpose(1, 0, 2)
        return pieces

    qkv_pieces = jnp.concatenate(
        [shuffle(query_proj, kvh), shuffle(key_proj, kvh), shuffle(value_proj, kvh)], axis=-1
    )
    qkv_pieces = jnp.tile(qkv_pieces, (cp // kvh, 1, 1))
    qkv = lax.all_to_all(qkv_pieces, "cp", 0, 0, tiled=True).reshape(cp * wrows, -1)
    qkv = lax.all_gather(qkv, "dp", axis=0, tiled=True)

    def to_columns(weight):
        pieces = weight.reshape(wrows, dp, cp, ffs).transpose(2, 0, 1, 3).reshape(cp, wrows, dp * ffs)
        return pieces

    gu = jnp.concatenate([to_columns(gate_proj), to_columns(up_proj)], axis=-1)
    gu = lax.all_to_all(gu, "cp", 0, 0, tiled=True).reshape(cp * wrows, -1)
    gu = lax.all_gather(gu, "dp", axis=0, tiled=True)
    half = dp * ffs
    gate_w, up_w = gu[:, :half], gu[:, half:]
    down_w = lax.all_gather(down_proj, "dp", axis=0, tiled=True)
    out_full = lax.all_gather(out_proj, both, axis=0, tiled=True)

    span_rows = length // span_order.shape[0]
    stored = jnp.arange(length, dtype=jnp.int32)
    places = span_order[stored // span_rows] * span_rows + stored % span_rows
    docs_seq = lax.dynamic_index_in_dim(segments.reshape(-1, length), my_seq, 0, keepdims=False)
    docs = jnp.take(docs_seq, places)
    doc_places = jnp.take(document_places(docs_seq), places)
    frequency = THETA ** (-jnp.arange(0, HD, 2).astype(F32) / HD)
    angles = doc_places.astype(F32)[:, None] * frequency
    allowed = (docs[:, None] == docs[None, :]) & (places[None, :] <= places[:, None])

    x_own = tokens.reshape(own, width)
    x_all = lax.all_gather(tokens.reshape(micros * seqs, rows, width), "cp", axis=1, tiled=True)
    x_seq = lax.dynamic_index_in_dim(x_all, my_seq, 0, keepdims=False).astype(F32)
    normed = rms_norm(x_seq, pre_full).astype(BF)
    raw = dot(normed, qkv)
    q_raw = raw[:, :qcols].reshape(length, group, HD)
    k_raw = raw[:, qcols : qcols + HD]
    v = raw[:, qcols + HD :].astype(BF)
    q_gain, k_gain = head_full[:HD], head_full[HD:]
    q_fun = lambda r, g: head_norm(r, g, angles[:, None, :])
    k_fun = lambda r, g: head_norm(r, g, angles)
    q, q_pull = jax.vjp(q_fun, q_raw, q_gain)
    k, k_pull = jax.vjp(k_fun, k_raw, k_gain)
    q = q.astype(BF).transpose(1, 0, 2)
    k = k.astype(BF)
    attended, log_total = attention_fwd(q, k, v, allowed)
    mixed_mine = attended.transpose(1, 0, 2).reshape(length, qcols).astype(BF)

    def to_tokens(a):
        a = lax.all_to_all(a.reshape(cp, rows, qcols), "cp", 0, 0, tiled=True)
        return a.reshape(micros * seqs, kvh, rows, qcols).transpose(0, 2, 1, 3).reshape(own, kvh * qcols)

    def to_heads(a):
        a = a.reshape(micros * seqs, rows, kvh, qcols).transpose(0, 2, 1, 3).reshape(cp, rows, qcols)
        return lax.all_to_all(a, "cp", 0, 0, tiled=True).reshape(length, qcols)

    mixed = to_tokens(mixed_mine)
    middle = x_own.astype(F32) + dot(mixed, out_full)
    normed_mid = rms_norm(middle, mid_full).astype(BF)

    cot_own = cotangent.reshape(own, width)
    c_all = lax.all_gather(cot_own, "cp", axis=0, tiled=True)
    nm_all = lax.all_gather(normed_mid, "cp", axis=0, tiled=True)
    gate = dot(nm_all, gate_w)
    up = dot(nm_all, up_w)
    sig = jax.nn.sigmoid(gate)
    act = gate * sig
    hidden = (act * up).astype(BF)
    out_part = dot(hidden, down_w).astype(BF)
    out_rows = lax.psum_scatter(out_part, "cp", scatter_dimension=0, tiled=True)
    block_out = (middle + out_rows.astype(F32)).astype(BF)

    grad_hidden = dot_nt(c_all, down_w)
    gg = (grad_hidden * up * sig * (1.0 + gate * (1.0 - sig))).astype(BF)
    gu_in = (grad_hidden * act).astype(BF)
    gnm_part = (dot_nt(gg, gate_w) + dot_nt(gu_in, up_w)).astype(BF)
    gnm = lax.psum_scatter(gnm_part, "cp", scatter_dimension=0, tiled=True).astype(F32)
    g_down = dot_tn(hidden, c_all)
    g_gate = dot_tn(nm_all, gg)
    g_up = dot_tn(nm_all, gu_in)

    g_down = lax.psum_scatter(g_down.astype(BF), "dp", scatter_dimension=0, tiled=True).astype(F32)
    g_gu = jnp.concatenate([g_gate, g_up], axis=-1).astype(BF)
    g_gu = lax.psum_scatter(g_gu, "dp", scatter_dimension=0, tiled=True)
    g_gu = lax.all_to_all(g_gu.reshape(cp, wrows, 2 * half), "cp", 0, 0, tiled=True).astype(F32)
    from_columns = lambda a: a.reshape(cp, wrows, dp, ffs).transpose(1, 2, 0, 3).reshape(wrows, -1)
    g_gate_own = from_columns(g_gu[..., :half])
    g_up_own = from_columns(g_gu[..., half:])

    unused, mid_pull = jax.vjp(rms_norm, middle, mid_full)
    part, g_mid = mid_pull(gnm)
    grad_middle = cot_own.astype(F32) + part
    branch = grad_middle.astype(BF)
    g_out = dot_tn(mixed, branch).astype(BF)
    g_out = lax.psum_scatter(g_out, both, scatter_dimension=0, tiled=True).astype(F32)
    grad_mixed = to_heads(dot_nt(branch, out_full).astype(BF))
    gm = grad_mixed.reshape(length, group, HD).transpose(1, 0, 2)
    delta = jnp.sum(gm.astype(F32) * attended, axis=-1, keepdims=True)
    grad_q, grad_k, grad_v = attention_bwd(q, k, v, allowed, log_total, delta, gm)
    gq_raw, gq_gain = q_pull(grad_q.transpose(1, 0, 2))
    gk_raw, gk_gain = k_pull(grad_k)
    low = jnp.concatenate([gq_raw.reshape(length, qcols), gk_raw, grad_v], axis=-1).astype(BF)
    g_qkv = dot_tn(normed, low).astype(BF)
    gn_part = dot_nt(low, qkv).astype(BF)
    onehot = (jnp.arange(micros * seqs) == my_seq).astype(BF)
    gn_wide = gn_part.reshape(cp, 1, rows, width) * onehot[None, :, None, None]
    gn = lax.psum_scatter(gn_wide.reshape(cp * own, width), "cp", scatter_dimension=0, tiled=True).astype(F32)
    unused, pre_pull = jax.vjp(rms_norm, x_own.astype(F32), pre_full)
    part, g_pre = pre_pull(gn)
    grad_tokens = grad_middle + part

    g_qkv = lax.psum_scatter(g_qkv, "dp", scatter_dimension=0, tiled=True)
    g_qkv = lax.all_to_all(g_qkv.reshape(cp, wrows, -1), "cp", 0, 0, tiled=True).astype(F32)
    g_qkv = g_qkv.reshape(micros * seqs, kvh, wrows, -1).sum(0)
    pick = lambda a: a.transpose(1, 0, 2).reshape(wrows, -1)
    g_query = pick(g_qkv[..., :qcols])
    g_key = pick(g_qkv[..., qcols : qcols + HD])
    g_value = pick(g_qkv[..., qcols + HD :])

    small = jnp.concatenate([
        g_pre.reshape(dp * cp, -1), g_mid.reshape(dp * cp, -1),
        jnp.concatenate([gq_gain, gk_gain]).reshape(dp * cp, -1)], axis=-1)
    small = lax.psum_scatter(small, both, scatter_dimension=0, tiled=True)[0]
    return (
        block_out.reshape(tokens.shape), grad_tokens.reshape(tokens.shape),
        small[:wrows], g_query, g_key, g_value, small[2 * wrows :], g_out,
        small[wrows : 2 * wrows], g_gate_own, g_up_own, g_down,
    )


def solution(mesh):
    both = ("dp", "cp")
    act = P(None, "dp", "cp", None)
    mat, vec = P(both, None), P(both)
    return jax.shard_map(
        local,
        mesh=mesh,
        in_specs=(act, act, P(None, "dp", None), P(), vec, mat, mat, mat, vec, mat, vec, mat, mat, mat),
        out_specs=(act, act, vec, mat, mat, mat, vec, mat, vec, mat, mat, mat),
        check_vma=False,
    )
```

```python
import jax
import jax.numpy as jnp
from jax import lax
from jax.experimental import pallas as pl
from jax.experimental.pallas import tpu as pltpu
from jax.sharding import PartitionSpec as P

MESH = pl.DeviceIdType.MESH

HD = 64
EPS = 1e-05
THETA = 1000000.0
BF = jnp.bfloat16
F32 = jnp.float32


def rms_norm(values, gain):
    return values * lax.rsqrt(jnp.mean(values * values, axis=-1, keepdims=True) + EPS) * gain


def rotate(values, angles):
    half = values.shape[-1] // 2
    a, b = values[..., :half], values[..., half:]
    cosine, sine = jnp.cos(angles), jnp.sin(angles)
    return jnp.concatenate([a * cosine - b * sine, b * cosine + a * sine], axis=-1)


def document_places(doc_ids):
    length = doc_ids.shape[-1]
    indices = jnp.arange(length, dtype=jnp.int32)
    changed = jnp.concatenate([jnp.ones((1,), jnp.bool_), doc_ids[1:] != doc_ids[:-1]])
    starts = lax.cummax(jnp.where(changed, indices, 0), axis=0)
    return indices - starts


def dot(a, b):
    return jnp.dot(a, b, preferred_element_type=F32)


def dot_nt(a, b):
    return lax.dot_general(a, b, (((1,), (1,)), ((), ())), preferred_element_type=F32)


def dot_tn(a, b):
    return lax.dot_general(a, b, (((0,), (0,)), ((), ())), preferred_element_type=F32)


def attention_fwd(q, k, v, allowed):
    scores = jnp.einsum("gqd,kd->gqk", q, k, preferred_element_type=F32) * HD**-0.5
    masked = jnp.where(allowed[None], scores, -1e30)
    top = jnp.max(masked, axis=-1, keepdims=True)
    unscaled = jnp.exp(masked - top)
    total = jnp.sum(unscaled, axis=-1, keepdims=True)
    attended = jnp.einsum("gqk,kd->gqd", unscaled.astype(BF), v, preferred_element_type=F32) / total
    return attended, top + jnp.log(total)


def attention_bwd(q, k, v, allowed, log_total, delta, gm):
    scores = jnp.einsum("gqd,kd->gqk", q, k, preferred_element_type=F32) * HD**-0.5
    prob = jnp.exp(jnp.where(allowed[None], scores, -1e30) - log_total)
    grad_v = jnp.einsum("gqk,gqd->kd", prob.astype(BF), gm, preferred_element_type=F32)
    grad_prob = jnp.einsum("gqd,kd->gqk", gm, v, preferred_element_type=F32)
    gs = (prob * (grad_prob - delta)).astype(BF)
    grad_q = jnp.einsum("gqk,kd->gqd", gs, k, preferred_element_type=F32) * HD**-0.5
    grad_k = jnp.einsum("gqk,gqd->kd", gs, q, preferred_element_type=F32) * HD**-0.5
    return grad_q, grad_k, grad_v


def head_norm(raw, gain, angles):
    return rotate(rms_norm(raw, gain), angles)


def flip(bit):
    return 1 - bit


def ffn_kernel(nm_ref, c_ref, wg_ref, wu_ref, wd_ref, gnm_ref, out_ref, ggT_ref, guT_ref, gd_ref,
               nm, part, sib_in, y_in, z_in, hid, gg, gu,
               ag_ss, ag_sy, ag_su, ag_sd, ag_rs, ag_ry, ag_rz,
               rs_ss, rs_sy, rs_sz, rs_rs, rs_ry, rs_rz):
    dp = lax.axis_index("dp")
    me = lax.axis_index("cp")
    z, y, k = me // 4, (me // 2) % 2, me % 2
    upper = z // 2
    w = z + upper * (3 - 2 * z)
    rows = nm_ref.shape[0]

    def dev(zz, yy, kk):
        return (dp, zz * 4 + yy * 2 + kk)

    sib, ynb = dev(z, y, 1 - k), dev(z, 1 - y, k)

    def order(j):
        first = (3 - j) // 3
        second = (j % 2) * ((3 - j) // 2)
        near = j + w * first - w * second
        return near + upper * (3 - 2 * near)

    def remote(src, dst, ssem, rsem, to):
        return pltpu.make_async_remote_copy(
            src_ref=src, dst_ref=dst, send_sem=ssem, recv_sem=rsem, device_id=to, device_id_type=MESH
        )

    def ag_sib(zs, dy):
        b = nm.at[zs, y + dy * (1 - 2 * y), k]
        return remote(b, b, ag_ss.at[zs, dy], ag_rs.at[zs, dy], sib)

    def ag_y(zs):
        b = nm.at[zs, y, k]
        return remote(b, b, ag_sy.at[zs], ag_ry.at[zs], ynb)

    def ag_up(zs):
        b = nm.at[zs, y, k]
        return remote(b, b, ag_su.at[zs], ag_rz.at[zs], dev(z + 1, y, k))

    def ag_down(zs):
        b = nm.at[zs, y, k]
        return remote(b, b, ag_sd.at[zs], ag_rz.at[zs], dev(z - 1, y, k))

    def rs_sib(zs, dy):
        return remote(part.at[zs, dy, 1 - k], sib_in.at[zs, dy], rs_ss.at[zs, dy], rs_rs.at[zs, dy], sib)

    def rs_y(zs):
        return remote(part.at[zs, 1, k], y_in.at[zs], rs_sy.at[zs], rs_ry.at[zs], ynb)

    def rs_z(zs):
        return remote(part.at[zs, 0, k], z_in.at[z], rs_sz.at[zs], rs_rz.at[z], dev(zs, y, k))

    def rs_z_wait(zs):
        remote(part.at[zs, 0, k], z_in.at[zs], rs_sz.at[zs], rs_rz.at[zs], sib).wait_recv()

    nm[z, y, k] = nm_ref[...]
    barrier = pltpu.get_barrier_semaphore()
    peers = [sib, ynb] + [dev((z + r) % 4, y, k) for r in range(1, 4)]
    for p in peers:
        pl.semaphore_signal(barrier, inc=1, device_id=p, device_id_type=MESH)
    pl.semaphore_wait(barrier, len(peers))

    def compute(zs, dy):
        ys = y + dy * (1 - 2 * y)
        a = nm[zs, ys].reshape(2 * rows, -1)
        c = c_ref[zs, ys].reshape(2 * rows, -1)
        gate = dot(a, wg_ref[...])
        up = dot(a, wu_ref[...])
        gh = dot_nt(c, wd_ref[...])
        sig = 1.0 / (1.0 + jnp.exp(-gate))
        act = gate * sig
        h = (act * up).astype(BF)
        g1 = (gh * up * sig * (1.0 + gate * (1.0 - sig))).astype(BF)
        g2 = (gh * act).astype(BF)
        hid[zs, ys] = h
        gg[zs, ys] = g1
        gu[zs, ys] = g2
        part[zs, dy] = (dot_nt(g1, wg_ref[...]) + dot_nt(g2, wu_ref[...])).astype(BF).reshape(2, rows, -1)
        out_ref[zs, ys] = dot(h, wd_ref[...]).astype(BF).reshape(2, rows, -1)

    def add_sib(zs, dy):
        rs_sib(zs, dy).wait_recv()
        part[zs, dy, k] = (part[zs, dy, k].astype(F32) + sib_in[zs, dy].astype(F32)).astype(BF)

    def add_y(zs):
        rs_y(zs).wait_recv()
        part[zs, 0, k] = (part[zs, 0, k].astype(F32) + y_in[zs].astype(F32)).astype(BF)

    ag_sib(z, 0).start()
    ag_y(z).start()

    @pl.when(z < 3)
    def _():
        ag_up(z).start()

    @pl.when(z > 0)
    def _():
        ag_down(z).start()

    def body(j, carry):
        zs = order(j)
        zp = order(j - 1 + (3 - j) // 3)

        @pl.when(j > 0)
        def _():
            remote(nm.at[zs, y, k], nm.at[zs, y, k], ag_su.at[zs], ag_rz.at[zs], sib).wait_recv()
            ag_y(zs).start()
            ag_sib(zs, 0).start()

            @pl.when((zs < z) & (z < 3))
            def _():
                ag_up(zs).start()

            @pl.when((zs > z) & (z > 0))
            def _():
                ag_down(zs).start()

        ag_sib(zs, 0).wait_recv()
        compute(zs, 0)
        rs_sib(zs, 0).start()

        @pl.when(j > 0)
        def _():
            add_sib(zp, 1)
            rs_y(zp).start()

        ag_y(zs).wait_recv()
        ag_sib(zs, 1).start()
        ag_sib(zs, 1).wait_recv()
        compute(zs, 1)
        rs_sib(zs, 1).start()
        add_sib(zs, 0)

        @pl.when(j > 0)
        def _():
            add_y(zp)

            @pl.when(zp != z)
            def _():
                rs_z(zp).start()

        return carry

    lax.fori_loop(0, 4, body, 0)
    last = order(3)
    add_sib(last, 1)
    rs_y(last).start()
    full = 16 * rows
    gd_ref[...] = dot_tn(hid[...].reshape(full, -1), c_ref[...].reshape(full, -1)).astype(BF)
    add_y(last)
    rs_z(last).start()
    ggT_ref[...] = dot_tn(gg[...].reshape(full, -1), nm[...].reshape(full, -1)).astype(BF)
    guT_ref[...] = dot_tn(gu[...].reshape(full, -1), nm[...].reshape(full, -1)).astype(BF)
    total = part[z, 0, k].astype(F32)
    for j in range(1, 4):
        rs_z_wait(order(j))
        total = total + z_in[order(j)].astype(F32)
    gnm_ref[...] = total
    for j in range(4):
        zs = order(j)
        ag_y(zs).wait_send()
        rs_y(zs).wait_send()
        for dy in range(2):
            ag_sib(zs, dy).wait_send()
            rs_sib(zs, dy).wait_send()
        if j:
            rs_z(zs).wait_send()

        @pl.when((zs <= z) & (z < 3))
        def _():
            ag_up(zs).wait_send()

        @pl.when((zs >= z) & (z > 0))
        def _():
            ag_down(zs).wait_send()


def ffn_call(nm_own, c_all, wg, wu, wd):
    rows, width = nm_own.shape
    ff = wd.shape[0]
    vm = pl.BlockSpec(memory_space=pltpu.VMEM)
    dma = pltpu.SemaphoreType.DMA
    return pl.pallas_call(
        ffn_kernel,
        out_shape=(
            jax.ShapeDtypeStruct((rows, width), F32),
            jax.ShapeDtypeStruct((4, 2, 2, rows, width), BF),
            jax.ShapeDtypeStruct((ff, width), BF),
            jax.ShapeDtypeStruct((ff, width), BF),
            jax.ShapeDtypeStruct((ff, width), BF),
        ),
        in_specs=[vm] * 5,
        out_specs=(vm,) * 5,
        scratch_shapes=[
            pltpu.VMEM((4, 2, 2, rows, width), BF),
            pltpu.VMEM((4, 2, 2, rows, width), BF),
            pltpu.VMEM((4, 2, rows, width), BF),
            pltpu.VMEM((4, rows, width), BF),
            pltpu.VMEM((4, rows, width), BF),
            pltpu.VMEM((4, 2, 2 * rows, ff), BF),
            pltpu.VMEM((4, 2, 2 * rows, ff), BF),
            pltpu.VMEM((4, 2, 2 * rows, ff), BF),
            dma((4, 2)), dma((4,)), dma((4,)), dma((4,)), dma((4, 2)), dma((4,)), dma((4,)),
            dma((4, 2)), dma((4,)), dma((4,)), dma((4, 2)), dma((4,)), dma((4,)),
        ],
        compiler_params=pltpu.CompilerParams(
            collective_id=0, has_side_effects=True, vmem_limit_bytes=60 << 20
        ),
        name="ffn",
    )(nm_own, c_all.reshape(4, 2, 2, rows, width), wg, wu, wd)


def local(tokens, cotangent, segments, span_order, pre_gain, query_proj, key_proj, value_proj,
          head_gain, out_proj, mid_gain, gate_proj, up_proj, down_proj):
    micros, seqs, rows, width = tokens.shape
    both = ("dp", "cp")
    cp = lax.axis_size("cp")
    dp = lax.axis_size("dp")
    me = lax.axis_index("cp")
    length = rows * cp
    kvh = key_proj.shape[1] // HD
    group = query_proj.shape[1] // key_proj.shape[1]
    qcols = group * HD
    wrows = gate_proj.shape[0]
    ffs = down_proj.shape[0]
    own = micros * seqs * rows
    my_seq, my_head = me // kvh, me % kvh

    packed = jnp.concatenate([pre_gain, mid_gain, head_gain])
    gains = lax.all_gather(packed, both, axis=0, tiled=False).astype(F32)
    pre_full = gains[:, :wrows].reshape(-1)
    mid_full = gains[:, wrows : 2 * wrows].reshape(-1)
    head_full = gains[:, 2 * wrows :].reshape(-1)

    def shuffle(weight, parts):
        pieces = weight.reshape(wrows, parts, -1).transpose(1, 0, 2)
        return pieces

    qkv_pieces = jnp.concatenate(
        [shuffle(query_proj, kvh), shuffle(key_proj, kvh), shuffle(value_proj, kvh)], axis=-1
    )
    qkv_pieces = jnp.tile(qkv_pieces, (cp // kvh, 1, 1))
    qkv = lax.all_to_all(qkv_pieces, "cp", 0, 0, tiled=True).reshape(cp * wrows, -1)
    qkv = lax.all_gather(qkv, "dp", axis=0, tiled=True)

    def to_columns(weight):
        pieces = weight.reshape(wrows, dp, cp, ffs).transpose(2, 0, 1, 3).reshape(cp, wrows, dp * ffs)
        return pieces

    gu = jnp.concatenate([to_columns(gate_proj), to_columns(up_proj)], axis=-1)
    gu = lax.all_to_all(gu, "cp", 0, 0, tiled=True).reshape(cp * wrows, -1)
    gu = lax.all_gather(gu, "dp", axis=0, tiled=True)
    half = dp * ffs
    gate_w, up_w = gu[:, :half], gu[:, half:]
    down_w = lax.all_gather(down_proj, "dp", axis=0, tiled=True)
    out_full = lax.all_gather(out_proj, both, axis=0, tiled=True)

    span_rows = length // span_order.shape[0]
    stored = jnp.arange(length, dtype=jnp.int32)
    places = span_order[stored // span_rows] * span_rows + stored % span_rows
    docs_seq = lax.dynamic_index_in_dim(segments.reshape(-1, length), my_seq, 0, keepdims=False)
    docs = jnp.take(docs_seq, places)
    doc_places = jnp.take(document_places(docs_seq), places)
    frequency = THETA ** (-jnp.arange(0, HD, 2).astype(F32) / HD)
    angles = doc_places.astype(F32)[:, None] * frequency
    allowed = (docs[:, None] == docs[None, :]) & (places[None, :] <= places[:, None])

    x_own = tokens.reshape(own, width)
    x_all = lax.all_gather(tokens.reshape(micros * seqs, rows, width), "cp", axis=1, tiled=True)
    x_seq = lax.dynamic_index_in_dim(x_all, my_seq, 0, keepdims=False).astype(F32)
    normed = rms_norm(x_seq, pre_full).astype(BF)
    raw = dot(normed, qkv)
    q_raw = raw[:, :qcols].reshape(length, group, HD)
    k_raw = raw[:, qcols : qcols + HD]
    v = raw[:, qcols + HD :].astype(BF)
    q_gain, k_gain = head_full[:HD], head_full[HD:]
    q_fun = lambda r, g: head_norm(r, g, angles[:, None, :])
    k_fun = lambda r, g: head_norm(r, g, angles)
    q, q_pull = jax.vjp(q_fun, q_raw, q_gain)
    k, k_pull = jax.vjp(k_fun, k_raw, k_gain)
    q = q.astype(BF).transpose(1, 0, 2)
    k = k.astype(BF)
    attended, log_total = attention_fwd(q, k, v, allowed)
    mixed_mine = attended.transpose(1, 0, 2).reshape(length, qcols).astype(BF)

    def to_tokens(a):
        a = lax.all_to_all(a.reshape(cp, rows, qcols), "cp", 0, 0, tiled=True)
        return a.reshape(micros * seqs, kvh, rows, qcols).transpose(0, 2, 1, 3).reshape(own, kvh * qcols)

    def to_heads(a):
        a = a.reshape(micros * seqs, rows, kvh, qcols).transpose(0, 2, 1, 3).reshape(cp, rows, qcols)
        return lax.all_to_all(a, "cp", 0, 0, tiled=True).reshape(length, qcols)

    mixed = to_tokens(mixed_mine)
    middle = x_own.astype(F32) + dot(mixed, out_full)
    normed_mid = rms_norm(middle, mid_full).astype(BF)

    cot_own = cotangent.reshape(own, width)
    c_all = lax.all_gather(cot_own, "cp", axis=0, tiled=True)
    gnm, out_part, ggT, guT, g_down = ffn_call(normed_mid, c_all, gate_w, up_w, down_w)
    out_rows = lax.psum_scatter(out_part.reshape(cp * own, width), "cp", scatter_dimension=0, tiled=True)
    block_out = (middle + out_rows.astype(F32)).astype(BF)

    g_down = lax.psum_scatter(g_down, "dp", scatter_dimension=0, tiled=True).astype(F32)
    g_gu = jnp.concatenate([ggT, guT], axis=0).T
    g_gu = lax.psum_scatter(g_gu, "dp", scatter_dimension=0, tiled=True)
    g_gu = lax.all_to_all(g_gu.reshape(cp, wrows, 2 * half), "cp", 0, 0, tiled=True).astype(F32)
    from_columns = lambda a: a.reshape(cp, wrows, dp, ffs).transpose(1, 2, 0, 3).reshape(wrows, -1)
    g_gate_own = from_columns(g_gu[..., :half])
    g_up_own = from_columns(g_gu[..., half:])

    unused, mid_pull = jax.vjp(rms_norm, middle, mid_full)
    part, g_mid = mid_pull(gnm)
    grad_middle = cot_own.astype(F32) + part
    branch = grad_middle.astype(BF)
    g_out = dot_tn(mixed, branch).astype(BF)
    g_out = lax.psum_scatter(g_out, both, scatter_dimension=0, tiled=True).astype(F32)
    grad_mixed = to_heads(dot_nt(branch, out_full).astype(BF))
    gm = grad_mixed.reshape(length, group, HD).transpose(1, 0, 2)
    delta = jnp.sum(gm.astype(F32) * attended, axis=-1, keepdims=True)
    grad_q, grad_k, grad_v = attention_bwd(q, k, v, allowed, log_total, delta, gm)
    gq_raw, gq_gain = q_pull(grad_q.transpose(1, 0, 2))
    gk_raw, gk_gain = k_pull(grad_k)
    low = jnp.concatenate([gq_raw.reshape(length, qcols), gk_raw, grad_v], axis=-1).astype(BF)
    g_qkv = dot_tn(normed, low).astype(BF)
    gn_part = dot_nt(low, qkv).astype(BF)
    onehot = (jnp.arange(micros * seqs) == my_seq).astype(BF)
    gn_wide = gn_part.reshape(cp, 1, rows, width) * onehot[None, :, None, None]
    gn = lax.psum_scatter(gn_wide.reshape(cp * own, width), "cp", scatter_dimension=0, tiled=True).astype(F32)
    unused, pre_pull = jax.vjp(rms_norm, x_own.astype(F32), pre_full)
    part, g_pre = pre_pull(gn)
    grad_tokens = grad_middle + part

    g_qkv = lax.psum_scatter(g_qkv, "dp", scatter_dimension=0, tiled=True)
    g_qkv = lax.all_to_all(g_qkv.reshape(cp, wrows, -1), "cp", 0, 0, tiled=True).astype(F32)
    g_qkv = g_qkv.reshape(micros * seqs, kvh, wrows, -1).sum(0)
    pick = lambda a: a.transpose(1, 0, 2).reshape(wrows, -1)
    g_query = pick(g_qkv[..., :qcols])
    g_key = pick(g_qkv[..., qcols : qcols + HD])
    g_value = pick(g_qkv[..., qcols + HD :])

    small = jnp.concatenate([
        g_pre.reshape(dp * cp, -1), g_mid.reshape(dp * cp, -1),
        jnp.concatenate([gq_gain, gk_gain]).reshape(dp * cp, -1)], axis=-1)
    small = lax.psum_scatter(small, both, scatter_dimension=0, tiled=True)[0]
    return (
        block_out.reshape(tokens.shape), grad_tokens.reshape(tokens.shape),
        small[:wrows], g_query, g_key, g_value, small[2 * wrows :], g_out,
        small[wrows : 2 * wrows], g_gate_own, g_up_own, g_down,
    )


def solution(mesh):
    both = ("dp", "cp")
    act = P(None, "dp", "cp", None)
    mat, vec = P(both, None), P(both)
    return jax.shard_map(
        local,
        mesh=mesh,
        in_specs=(act, act, P(None, "dp", None), P(), vec, mat, mat, mat, vec, mat, vec, mat, mat, mat),
        out_specs=(act, act, vec, mat, mat, mat, vec, mat, vec, mat, mat, mat),
        check_vma=False,
    )
```

```python
import jax
import jax.numpy as jnp
from jax import lax
from jax.experimental import pallas as pl
from jax.experimental.pallas import tpu as pltpu
from jax.sharding import PartitionSpec as P

MESH = pl.DeviceIdType.MESH

HD = 64
EPS = 1e-05
THETA = 1000000.0
BF = jnp.bfloat16
F32 = jnp.float32


def rms_norm(values, gain):
    return values * lax.rsqrt(jnp.mean(values * values, axis=-1, keepdims=True) + EPS) * gain


def dot(a, b):
    return jnp.dot(a, b, preferred_element_type=F32)


def dot_nt(a, b):
    return lax.dot_general(a, b, (((1,), (1,)), ((), ())), preferred_element_type=F32)


def dot_tn(a, b):
    return lax.dot_general(a, b, (((0,), (0,)), ((), ())), preferred_element_type=F32)


class Place:
    def __init__(self):
        self.dp = lax.axis_index("dp")
        self.dps = lax.axis_size("dp")
        self.me = lax.axis_index("cp")
        self.z, self.y, self.k = self.me // 4, (self.me // 2) % 2, self.me % 2
        self.upper = self.z // 2
        self.w = self.z + self.upper * (3 - 2 * self.z)
        self.sib = self.dev(self.z, self.y, 1 - self.k)
        self.ynb = self.dev(self.z, 1 - self.y, self.k)

    def dev(self, z, y, k):
        return (self.dp, z * 4 + y * 2 + k)

    def order(self, j):
        near = [self.w, 1 - self.w, 2, 3][j]
        return near + self.upper * (3 - 2 * near)


def remote(src, dst, ssem, rsem, to):
    return pltpu.make_async_remote_copy(
        src_ref=src, dst_ref=dst, send_sem=ssem, recv_sem=rsem, device_id=to, device_id_type=MESH
    )


def greet(peers):
    barrier = pltpu.get_barrier_semaphore()
    for p in peers:
        pl.semaphore_signal(barrier, inc=1, device_id=p, device_id_type=MESH)
    pl.semaphore_wait(barrier, len(peers))


def group_peers(at):
    return [(at.dp, (at.me + r) % 16) for r in range(1, 16)] + [
        ((at.dp + r) % at.dps, at.me) for r in range(1, at.dps)
    ]


class Exchange:
    def __init__(self, at, source, dest, ss, rs, xs, xr):
        self.at, self.source, self.dest = at, source, dest
        self.ss, self.rs, self.xs, self.xr = ss, rs, xs, xr

    def push(self, r):
        at = self.at
        to = (at.me + r) % 16
        return remote(self.source(to), self.dest.at[at.dp, at.me], self.ss.at[r], self.rs.at[at.me], (at.dp, to))

    def arrival(self, s):
        b = self.dest.at[self.at.dp, s]
        return remote(b, b, self.ss.at[0], self.rs.at[s], self.at.sib)

    def onward(self, s, r):
        at = self.at
        b = self.dest.at[at.dp, s]
        return remote(b, b, self.xs.at[r, s], self.xr.at[at.dp, s], ((at.dp + r) % at.dps, at.me))

    def onward_arrival(self, s, r):
        d = (self.at.dp + r) % self.at.dps
        b = self.dest.at[d, s]
        return remote(b, b, self.xs.at[0, s], self.xr.at[d, s], self.at.sib)

    def start(self):
        lax.fori_loop(1, 16, lambda r, c: (self.push(r).start(), c)[1], 0)
        at = self.at
        for r in range(1, at.dps):
            self.own_onward(r).start()

    def own_onward(self, r):
        at = self.at
        return remote(self.source(at.me), self.dest.at[at.dp, at.me], self.xs.at[r, at.me],
                      self.xr.at[at.dp, at.me], ((at.dp + r) % at.dps, at.me))

    def forward(self, lo, hi):
        def step(r, c):
            s = (self.at.me + 16 - r) % 16
            self.arrival(s).wait_recv()
            for q in range(1, self.at.dps):
                self.onward(s, q).start()
            return c

        lax.fori_loop(lo, hi, step, 0)

    def finish(self):
        at = self.at

        def step(s, c):
            for q in range(1, at.dps):
                self.onward_arrival(s, q).wait_recv()
                self.onward(s, q).wait_send()
            return c

        lax.fori_loop(0, 16, step, 0)
        lax.fori_loop(1, 16, lambda r, c: (self.push(r).wait_send(), c)[1], 0)


class Spread:
    def __init__(self, at, buf, own, half, ss, sy, sz, rs, ry, rz):
        self.at, self.buf, self.own, self.half = at, buf, own, half
        self.ss, self.sy, self.sz, self.rs, self.ry, self.rz = ss, sy, sz, rs, ry, rz

    def sib_copy(self, zs, ys, src=None):
        at = self.at
        b = self.buf.at[zs, ys, at.k]
        return remote(b if src is None else src, b, self.ss.at[zs, ys], self.rs.at[zs, ys], at.sib)

    def y_copy(self, zs, src=None):
        at = self.at
        b = self.buf.at[zs, at.y, at.k]
        return remote(b if src is None else src, b, self.sy.at[zs], self.ry.at[zs], at.ynb)

    def z_copy(self, zt):
        at = self.at
        b = self.buf.at[at.z, at.y, at.k]
        return remote(self.own(zt), b, self.sz.at[zt], self.rz.at[at.z], at.dev(zt, at.y, at.k))

    def start(self):
        at = self.at
        mine = self.own(at.z)
        for j in range(1, 4):
            self.z_copy(at.order(j)).start()
        self.y_copy(at.z, mine).start()
        self.sib_copy(at.z, at.y, mine).start()

    def z_arrive(self, j):
        at = self.at
        zs = at.order(j)
        b = self.buf.at[zs, at.y, at.k]
        remote(b, b, self.sz.at[zs], self.rz.at[zs], at.sib).wait_recv()
        self.y_copy(zs).start()
        self.sib_copy(zs, at.y).start()

    def y_arrive(self, j):
        at = self.at
        zs = at.order(j)
        b = self.buf.at[zs, 1 - at.y, at.k]
        remote(b, b, self.sy.at[zs], self.ry.at[zs], at.sib).wait_recv()
        self.sib_copy(zs, 1 - at.y).start()

    def finish(self):
        at = self.at
        for j in range(4):
            zs = at.order(j)
            for ys in range(2):
                b = self.buf.at[zs, ys, 1 - at.k]
                remote(b, b, self.ss.at[zs, ys], self.rs.at[zs, ys], at.sib).wait_recv()
                self.sib_copy(zs, ys).wait_send()
            self.y_copy(zs).wait_send()
            if j:
                self.z_copy(zs).wait_send()


def start_kernel(x_ref, c_ref, query_ref, key_ref, value_ref, gate_ref, up_ref, down_ref, gain_ref,
                 xs_ref, ca_ref, qa_ref, ga_ref, da_ref, na_ref,
                 x0, x1, x2, x3, x4, x5, c0, c1, c2, c3, c4, c5,
                 q0, q1, q2, q3, g0, g1, g2, g3, n0, n1, n2, n3, d0, d1, lsem, qkv_ref, gu_ref):
    at = Place()
    dps = at.dps
    kvh = qkv_ref.shape[0]
    greet(group_peers(at))
    xs = Spread(at, xs_ref, lambda zt: x_ref.at[zt // 2], True, x0, x1, x2, x3, x4, x5)
    ca = Spread(at, ca_ref, lambda zt: c_ref, False, c0, c1, c2, c3, c4, c5)
    qa = Exchange(at, lambda to: qkv_ref.at[to % kvh], qa_ref, q0, q1, q2, q3)
    ga = Exchange(at, lambda to: gu_ref.at[to], ga_ref, g0, g1, g2, g3)
    na = Exchange(at, lambda to: gain_ref, na_ref, n0, n1, n2, n3)
    xs.start()
    na.start()
    qc = query_ref.shape[1] // kvh
    for h in range(kvh):
        qkv_ref[h, :, :qc] = query_ref[:, h * qc : (h + 1) * qc]
        qkv_ref[h, :, qc : qc + HD] = key_ref[:, h * HD : (h + 1) * HD]
        qkv_ref[h, :, qc + HD :] = value_ref[:, h * HD : (h + 1) * HD]
    qa.start()
    own = [
        pltpu.make_async_copy(x_ref.at[at.z // 2], xs_ref.at[at.z, at.y, at.k], lsem.at[0]),
        pltpu.make_async_copy(c_ref, ca_ref.at[at.z, at.y, at.k], lsem.at[1]),
        pltpu.make_async_copy(qkv_ref.at[at.me % kvh], qa_ref.at[at.dp, at.me], lsem.at[2]),
        pltpu.make_async_copy(gu_ref.at[at.me], ga_ref.at[at.dp, at.me], lsem.at[3]),
        pltpu.make_async_copy(down_ref, da_ref.at[at.dp], lsem.at[4]),
        pltpu.make_async_copy(gain_ref, na_ref.at[at.dp, at.me], lsem.at[5]),
    ]
    for c in own[:3] + own[4:]:
        c.start()
    padded, ffs = gu_ref.shape[2] // 2, down_ref.shape[0]
    for t in range(16):
        for base, ref in ((0, gate_ref), (padded, up_ref)):
            for d in range(dps):
                piece = ref[:, (d * 16 + t) * ffs : (d * 16 + t + 1) * ffs]
                gu_ref[t, :, base + d * ffs : base + (d + 1) * ffs] = piece
            if padded > dps * ffs:
                gu_ref[t, :, base + dps * ffs : base + padded] = jnp.zeros((gu_ref.shape[1], padded - dps * ffs), BF)
    own[3].start()
    xs.z_arrive(1)
    na.forward(1, 16)
    xs.z_arrive(2)
    xs.y_arrive(0)
    xs.z_arrive(3)
    qa.forward(1, 16)
    for j in range(1, 4):
        xs.y_arrive(j)
    down = [
        remote(down_ref, da_ref.at[at.dp], d0.at[r], d1.at[at.dp], ((at.dp + r) % dps, at.me))
        for r in range(1, dps)
    ]
    ca.start()
    ga.start()
    for c in down:
        c.start()
    na.finish()
    qa.finish()
    xs.finish()
    ca.z_arrive(1)
    ca.y_arrive(0)
    ga.forward(1, 6)
    ca.z_arrive(2)
    ca.y_arrive(1)
    ga.forward(6, 11)
    ca.z_arrive(3)
    ca.y_arrive(2)
    ga.forward(11, 16)
    ca.y_arrive(3)
    ca.finish()
    ga.finish()
    for r in range(1, dps):
        d = (at.dp + r) % dps
        remote(da_ref.at[d], da_ref.at[d], d0.at[0], d1.at[d], at.sib).wait_recv()
    for c in down:
        c.wait_send()
    for c in own:
        c.wait()


def start_call(x_own, c_own, query, key, value, gate, up, down, gain):
    dps = lax.axis_size("dp")
    rows, width = c_own.shape
    kvh, wrows = key.shape[1] // HD, key.shape[0]
    cols = query.shape[1] // kvh + 2 * HD
    padded = -(-dps * down.shape[0] // 128) * 128
    any_ = pl.BlockSpec(memory_space=pl.ANY)
    vm = pl.BlockSpec(memory_space=pltpu.VMEM)
    dma = pltpu.SemaphoreType.DMA
    spread = [dma((4, 2)), dma((4,)), dma((4,)), dma((4, 2)), dma((4,)), dma((4,))]
    exchange = [dma((16,)), dma((16,)), dma((dps, 16)), dma((dps, 16))]
    sds = jax.ShapeDtypeStruct
    return pl.pallas_call(
        start_kernel,
        out_shape=(
            sds((4, 2, 2) + x_own.shape[1:], BF),
            sds((4, 2, 2, rows, width), BF),
            sds((dps, 16, wrows, cols), BF),
            sds((dps, 16, wrows, 2 * padded), BF),
            sds((dps,) + down.shape, BF),
            sds((dps, 16) + gain.shape, F32),
        ),
        in_specs=[any_, any_, vm, vm, vm, vm, vm, any_, any_],
        out_specs=(any_,) * 6,
        scratch_shapes=spread * 2 + exchange * 3 + [
            dma((dps,)), dma((dps,)), dma((6,)),
            pltpu.VMEM((kvh, wrows, cols), BF), pltpu.VMEM((16, wrows, 2 * padded), BF),
        ],
        compiler_params=pltpu.CompilerParams(
            collective_id=1, has_side_effects=True, vmem_limit_bytes=32 << 20
        ),
        name="start",
    )(x_own, c_own, query, key, value, gate, up, down, gain)


def ffn_kernel(nm_ref, c_ref, wgu_ref, wd_ref, gnm_ref, out_ref, ggu_ref, gd_ref,
               nm, part, sib_in, y_in, z_in, hid, dgu, wd,
               ag_ss, ag_sy, ag_su, ag_sd, ag_rs, ag_ry, ag_rz,
               rs_ss, rs_sy, rs_sz, rs_rs, rs_ry, rs_rz):
    dp = lax.axis_index("dp")
    me = lax.axis_index("cp")
    z, y, k = me // 4, (me // 2) % 2, me % 2
    upper = z // 2
    w = z + upper * (3 - 2 * z)
    rows = nm_ref.shape[0]

    def dev(zz, yy, kk):
        return (dp, zz * 4 + yy * 2 + kk)

    sib, ynb = dev(z, y, 1 - k), dev(z, 1 - y, k)

    def order(j):
        first = (3 - j) // 3
        second = (j % 2) * ((3 - j) // 2)
        near = j + w * first - w * second
        return near + upper * (3 - 2 * near)

    def remote(src, dst, ssem, rsem, to):
        return pltpu.make_async_remote_copy(
            src_ref=src, dst_ref=dst, send_sem=ssem, recv_sem=rsem, device_id=to, device_id_type=MESH
        )

    def ag_sib(zs, dy):
        b = nm.at[zs, y + dy * (1 - 2 * y), k]
        return remote(b, b, ag_ss.at[zs, dy], ag_rs.at[zs, dy], sib)

    def ag_y(zs):
        b = nm.at[zs, y, k]
        return remote(b, b, ag_sy.at[zs], ag_ry.at[zs], ynb)

    def ag_up(zs):
        b = nm.at[zs, y, k]
        return remote(b, b, ag_su.at[zs], ag_rz.at[zs], dev(z + 1, y, k))

    def ag_down(zs):
        b = nm.at[zs, y, k]
        return remote(b, b, ag_sd.at[zs], ag_rz.at[zs], dev(z - 1, y, k))

    def rs_sib(zs, dy):
        return remote(part.at[zs, dy, 1 - k], sib_in.at[zs, dy], rs_ss.at[zs, dy], rs_rs.at[zs, dy], sib)

    def rs_y(zs):
        return remote(part.at[zs, 1, k], y_in.at[zs], rs_sy.at[zs], rs_ry.at[zs], ynb)

    def rs_z(zs):
        return remote(part.at[zs, 0, k], z_in.at[z], rs_sz.at[zs], rs_rz.at[z], dev(zs, y, k))

    def rs_z_wait(zs):
        remote(part.at[zs, 0, k], z_in.at[zs], rs_sz.at[zs], rs_rz.at[zs], sib).wait_recv()

    ff, padded = wd_ref.shape[0], wd.shape[0]
    nm[z, y, k] = nm_ref[...]
    wd[pl.ds(0, ff), :] = wd_ref[...]
    if padded > ff:
        wd[pl.ds(ff, padded - ff), :] = jnp.zeros((padded - ff, wd.shape[1]), BF)
    barrier = pltpu.get_barrier_semaphore()
    peers = [sib, ynb] + [dev((z + r) % 4, y, k) for r in range(1, 4)]
    for p in peers:
        pl.semaphore_signal(barrier, inc=1, device_id=p, device_id_type=MESH)
    pl.semaphore_wait(barrier, len(peers))

    def compute(zs, dy):
        ys = y + dy * (1 - 2 * y)
        a = nm[zs, ys].reshape(2 * rows, -1)
        c = c_ref[zs, ys].reshape(2 * rows, -1)
        both = dot(a, wgu_ref[...])
        gate, up = both[:, :padded], both[:, padded:]
        gh = dot_nt(c, wd[...])
        sig = 1.0 / (1.0 + jnp.exp(-gate))
        act = gate * sig
        h = (act * up).astype(BF)
        hid[zs, ys] = h
        dgu[zs, ys, :, :padded] = (gh * up * sig * (1.0 + gate * (1.0 - sig))).astype(BF)
        dgu[zs, ys, :, padded:] = (gh * act).astype(BF)
        part[zs, dy] = dot_nt(dgu[zs, ys], wgu_ref[...]).astype(BF).reshape(2, rows, -1)
        out_ref[zs, ys] = dot(h, wd[...]).astype(BF).reshape(2, rows, -1)

    def add_sib(zs, dy):
        rs_sib(zs, dy).wait_recv()
        part[zs, dy, k] = (part[zs, dy, k].astype(F32) + sib_in[zs, dy].astype(F32)).astype(BF)

    def add_y(zs):
        rs_y(zs).wait_recv()
        part[zs, 0, k] = (part[zs, 0, k].astype(F32) + y_in[zs].astype(F32)).astype(BF)

    ag_sib(z, 0).start()
    ag_y(z).start()

    @pl.when(z < 3)
    def _():
        ag_up(z).start()

    @pl.when(z > 0)
    def _():
        ag_down(z).start()

    def body(j, carry):
        zs = order(j)
        zp = order(j - 1 + (3 - j) // 3)
        zn = order(j + 1 - j // 3)
        ag_sib(zs, 0).wait_recv()
        compute(zs, 0)
        rs_sib(zs, 0).start()

        @pl.when(j < 3)
        def _():
            remote(nm.at[zn, y, k], nm.at[zn, y, k], ag_su.at[zn], ag_rz.at[zn], sib).wait_recv()
            ag_y(zn).start()
            ag_sib(zn, 0).start()

            @pl.when((zn < z) & (z < 3))
            def _():
                ag_up(zn).start()

            @pl.when((zn > z) & (z > 0))
            def _():
                ag_down(zn).start()

        @pl.when(j > 0)
        def _():
            add_sib(zp, 1)
            rs_y(zp).start()

        ag_y(zs).wait_recv()
        ag_sib(zs, 1).start()
        ag_sib(zs, 1).wait_recv()
        compute(zs, 1)
        rs_sib(zs, 1).start()
        add_sib(zs, 0)

        @pl.when(j > 0)
        def _():
            add_y(zp)

            @pl.when(zp != z)
            def _():
                rs_z(zp).start()

        return carry

    lax.fori_loop(0, 4, body, 0)
    last = order(3)
    add_sib(last, 1)
    rs_y(last).start()
    full = 16 * rows

    def down_rows(i, carry):
        at = pl.ds(pl.multiple_of(i * 128, 128), 128)
        gd_ref[at, :] = dot_tn(hid[:, :, :, at].reshape(full, 128), c_ref[...].reshape(full, -1)).astype(BF)
        return carry

    lax.fori_loop(0, padded // 128, down_rows, 0)
    add_y(last)
    rs_z(last).start()

    def gate_rows(i, carry):
        at = pl.ds(pl.multiple_of(i * 256, 256), 256)
        ggu_ref[at, :] = dot_tn(nm[:, :, :, :, at].reshape(full, 256), dgu[...].reshape(full, -1)).astype(BF)
        return carry

    lax.fori_loop(0, nm.shape[-1] // 256, gate_rows, 0)
    total = part[z, 0, k].astype(F32)
    for j in range(1, 4):
        rs_z_wait(order(j))
        total = total + z_in[order(j)].astype(F32)
    gnm_ref[...] = total
    for j in range(4):
        zs = order(j)
        ag_y(zs).wait_send()
        rs_y(zs).wait_send()
        for dy in range(2):
            ag_sib(zs, dy).wait_send()
            rs_sib(zs, dy).wait_send()
        if j:
            rs_z(zs).wait_send()

        @pl.when((zs <= z) & (z < 3))
        def _():
            ag_up(zs).wait_send()

        @pl.when((zs >= z) & (z > 0))
        def _():
            ag_down(zs).wait_send()


def ffn_call(nm_own, c_all, wgu, wd):
    rows, width = nm_own.shape
    padded = wgu.shape[1] // 2
    vm = pl.BlockSpec(memory_space=pltpu.VMEM)
    dma = pltpu.SemaphoreType.DMA
    return pl.pallas_call(
        ffn_kernel,
        out_shape=(
            jax.ShapeDtypeStruct((rows, width), F32),
            jax.ShapeDtypeStruct((4, 2, 2, rows, width), BF),
            jax.ShapeDtypeStruct((width, 2 * padded), BF),
            jax.ShapeDtypeStruct((padded, width), BF),
        ),
        in_specs=[vm] * 4,
        out_specs=(vm,) * 4,
        scratch_shapes=[
            pltpu.VMEM((4, 2, 2, rows, width), BF),
            pltpu.VMEM((4, 2, 2, rows, width), BF),
            pltpu.VMEM((4, 2, rows, width), BF),
            pltpu.VMEM((4, rows, width), BF),
            pltpu.VMEM((4, rows, width), BF),
            pltpu.VMEM((4, 2, 2 * rows, padded), BF),
            pltpu.VMEM((4, 2, 2 * rows, 2 * padded), BF),
            pltpu.VMEM((padded, width), BF),
            dma((4, 2)), dma((4,)), dma((4,)), dma((4,)), dma((4, 2)), dma((4,)), dma((4,)),
            dma((4, 2)), dma((4,)), dma((4,)), dma((4, 2)), dma((4,)), dma((4,)),
        ],
        compiler_params=pltpu.CompilerParams(
            collective_id=0, has_side_effects=True, vmem_limit_bytes=56 << 20
        ),
        name="ffn",
    )(nm_own, c_all, wgu, wd)


class Collect:
    def __init__(self, at, part, own, sib_in, y_in, z_in, ls, ss, sy, sz, rs, ry, rz):
        self.at, self.part, self.own = at, part, own
        self.sib_in, self.y_in, self.z_in, self.ls = sib_in, y_in, z_in, ls
        self.ss, self.sy, self.sz, self.rs, self.ry, self.rz = ss, sy, sz, rs, ry, rz

    def sib_copy(self, zs, ys):
        at = self.at
        return remote(self.part.at[zs, ys, 1 - at.k], self.sib_in.at[zs, ys], self.ss.at[zs, ys], self.rs.at[zs, ys], at.sib)

    def load(self, zs, ys):
        return pltpu.make_async_copy(self.part.at[zs, ys, self.at.k], self.own.at[zs, ys], self.ls.at[zs, ys])

    def y_copy(self, zs):
        at = self.at
        return remote(self.own.at[zs, 1 - at.y], self.y_in.at[zs], self.sy.at[zs], self.ry.at[zs], at.ynb)

    def z_copy(self, zs):
        at = self.at
        return remote(self.own.at[zs, at.y], self.z_in.at[at.z], self.sz.at[zs], self.rz.at[at.z], at.dev(zs, at.y, at.k))

    def start(self):
        at = self.at
        for flip in range(2):
            ys = (1 - at.y) if flip == 0 else at.y
            for j in (3, 2, 1, 0):
                self.sib_copy(at.order(j), ys).start()
                self.load(at.order(j), ys).start()

    def add_sib(self, zs, ys):
        self.load(zs, ys).wait()
        self.sib_copy(zs, ys).wait_recv()
        self.own[zs, ys] = (self.own[zs, ys].astype(F32) + self.sib_in[zs, ys].astype(F32)).astype(BF)

    def sib_done(self, zs, ys):
        self.sib_copy(zs, ys).wait_send()

    def first(self, j):
        zs = self.at.order(j)
        self.add_sib(zs, 1 - self.at.y)
        self.y_copy(zs).start()

    def add_y(self, zs):
        at = self.at
        self.add_sib(zs, at.y)
        self.y_copy(zs).wait_recv()
        return (self.own[zs, at.y].astype(F32) + self.y_in[zs].astype(F32)).astype(BF)

    def second(self, j):
        at = self.at
        zs = at.order(j)
        total = self.add_y(zs)
        if j:
            self.own[zs, at.y] = total
            self.z_copy(zs).start()
        else:
            self.z_in[at.z] = total

    def finish(self):
        at = self.at
        for j in range(4):
            zs = at.order(j)
            if j:
                remote(self.own.at[zs, at.y], self.z_in.at[zs], self.sz.at[zs], self.rz.at[zs], at.sib).wait_recv()
                self.z_copy(zs).wait_send()
            self.y_copy(zs).wait_send()
            for ys in range(2):
                self.sib_done(zs, ys)


class CollectGroups(Collect):
    def __init__(self, *args):
        *args, self.whole, self.wide, self.sib_wide, self.x_in, self.lw, self.sw, self.rw, self.xs, self.xr = args
        super().__init__(*args)

    def pair(self, d, ys):
        at = self.at
        return remote(self.whole.at[d, ys, 1 - at.k], self.sib_wide.at[d, ys], self.sw.at[d, ys], self.rw.at[d, ys], at.sib)

    def pair_load(self, d, ys):
        return pltpu.make_async_copy(self.whole.at[d, ys, self.at.k], self.wide.at[d, ys], self.lw.at[d, ys])

    def across(self, r):
        at = self.at
        d = (at.dp + r) % at.dps
        return remote(self.wide.at[d], self.x_in.at[at.dp], self.xs.at[d], self.xr.at[at.dp], (d, at.me))

    def start(self):
        for d in range(self.at.dps):
            for ys in range(2):
                self.pair(d, ys).start()
                self.pair_load(d, ys).start()

    def middle(self):
        at = self.at
        for r in range(at.dps - 1, -1, -1):
            d = (at.dp + r) % at.dps
            for ys in range(2):
                self.pair_load(d, ys).wait()
                self.pair(d, ys).wait_recv()
                self.wide[d, ys] = (self.wide[d, ys].astype(F32) + self.sib_wide[d, ys].astype(F32)).astype(BF)
            if r:
                self.across(r).start()

    def join(self):
        at = self.at
        for r in range(1, at.dps):
            d = (at.dp + r) % at.dps
            remote(self.x_in.at[d], self.x_in.at[d], self.xs.at[d], self.xr.at[d], at.sib).wait_recv()
        for ys in range(2):
            total = self.wide[at.dp, ys].astype(F32)
            for r in range(1, at.dps):
                total = total + self.x_in[(at.dp + r) % at.dps, ys].astype(F32)
            for zs in range(4):
                self.own[zs, ys] = total[zs].astype(BF)

    def add_sib(self, zs, ys):
        pass

    def sib_done(self, zs, ys):
        pass

    def finish(self):
        super().finish()
        at = self.at
        for d in range(at.dps):
            for ys in range(2):
                self.pair(d, ys).wait_send()
        for r in range(1, at.dps):
            self.across(r).wait_send()


class ToOwners:
    def __init__(self, at, src, dst, ss, rs, part=None, x_in=None, xs=None, xr=None, ls=None):
        self.at, self.src, self.dst, self.ss, self.rs = at, src, dst, ss, rs
        self.part, self.x_in, self.xs, self.xr, self.ls = part, x_in, xs, xr, ls

    def across(self, r):
        at = self.at
        d = (at.dp + r) % at.dps
        return remote(self.part.at[d], self.x_in.at[at.dp], self.xs.at[d], self.xr.at[at.dp], (d, at.me))

    def load(self):
        return pltpu.make_async_copy(self.part.at[self.at.dp], self.src, self.ls.at[0])

    def sum_start(self):
        for r in range(1, self.at.dps):
            self.across(r).start()
        self.load().start()

    def sum_finish(self):
        at = self.at
        self.load().wait()
        total = self.src[...].astype(F32)
        for r in range(1, at.dps):
            d = (at.dp + r) % at.dps
            remote(self.x_in.at[d], self.x_in.at[d], self.xs.at[d], self.xr.at[d], at.sib).wait_recv()
            total = total + self.x_in[d].astype(F32)
        self.src[...] = total.astype(self.src.dtype)
        for r in range(1, at.dps):
            self.across(r).wait_send()

    def push(self, r):
        at = self.at
        to = (at.me + r) % 16
        return remote(self.src.at[to], self.dst.at[at.me], self.ss.at[r], self.rs.at[at.me], (at.dp, to))

    def own(self):
        return pltpu.make_async_copy(self.src.at[self.at.me], self.dst.at[self.at.me], self.ss.at[0])

    def start(self):
        lax.fori_loop(1, 16, lambda r, c: (self.push(r).start(), c)[1], 0)
        self.own().start()

    def finish(self):
        at = self.at

        def step(r, c):
            s = (at.me + 16 - r) % 16
            remote(self.dst.at[s], self.dst.at[s], self.ss.at[r], self.rs.at[s], at.sib).wait_recv()
            self.push(r).wait_send()
            return c

        lax.fori_loop(1, 16, step, 0)
        self.own().wait()


def finish_kernel(gn_ref, out_ref, go_ref, gu_ref, qkv_ref, gain_ref,
                  gn_sum, out_sum, go_sum, gate_sum, up_sum, query_sum, key_sum, value_sum, gain_sum,
                  a0, a1, a2, a3, b0, b1, b2, b3, c0, c1, c2, c3,
                  as0, as1, as2, as3, as4, as5, as6,
                  bs0, bs1, bs2, bs3, bs4, bs5, bs6,
                  cs0, cs1, cs2, cs3, cs4, cs5, cs6,
                  w0, w1, w2, ws0, ws1, ws2, ws3, ws4,
                  gu_in, us, ur,
                  q_mine, q_x, qkv_in, qs, qr, qxs, qxr, ql,
                  n_mine, n_x, n_in, ns, nr, nxs, nxr, nl):
    at = Place()
    greet(group_peers(at))
    gn = Collect(at, gn_ref, a0, a1, a2, a3, as0, as1, as2, as3, as4, as5, as6)
    out = Collect(at, out_ref, b0, b1, b2, b3, bs0, bs1, bs2, bs3, bs4, bs5, bs6)
    go = CollectGroups(at, None, c0, c1, c2, c3, cs0, cs1, cs2, cs3, cs4, cs5, cs6,
                       go_ref, w0, w1, w2, ws0, ws1, ws2, ws3, ws4)
    gu = ToOwners(at, gu_ref, gu_in, us, ur)
    qkv = ToOwners(at, q_mine, qkv_in, qs, qr, qkv_ref, q_x, qxs, qxr, ql)
    gain = ToOwners(at, n_mine, n_in, ns, nr, gain_ref, n_x, nxs, nxr, nl)
    gain.sum_start()
    qkv.sum_start()
    go.start()
    out.start()
    gn.start()
    gu.start()
    go.middle()
    gain.sum_finish()
    gain.start()
    out.first(3)
    gn.first(3)
    qkv.sum_finish()
    qkv.start()
    out.first(2)
    gn.first(2)
    out.first(1)
    gn.first(1)
    go.join()
    for j in (3, 2, 1):
        go.first(j)
    for tree in (out, gn, go):
        tree.first(0)
    for j in (3, 2, 1, 0):
        for tree in (out, gn, go):
            tree.second(j)
    gu.finish()
    wrows, padded, ffs = gu_in.shape[1], gu_in.shape[2] // 2, gate_sum.shape[1] // (16 * at.dps)
    for s in range(16):
        for base, ref in ((0, gate_sum), (padded, up_sum)):
            for d in range(at.dps):
                lo = base + d * ffs
                ref[:, (d * 16 + s) * ffs : (d * 16 + s + 1) * ffs] = gu_in[s, :, lo : lo + ffs].astype(F32)
    qkv.finish()
    kvh = key_sum.shape[1] // HD
    qc = query_sum.shape[1] // kvh
    for h in range(kvh):
        t = qkv_in[h].astype(F32)
        for m in range(1, 16 // kvh):
            t = t + qkv_in[m * kvh + h].astype(F32)
        query_sum[:, h * qc : (h + 1) * qc] = t[:, :qc]
        key_sum[:, h * HD : (h + 1) * HD] = t[:, qc : qc + HD]
        value_sum[:, h * HD : (h + 1) * HD] = t[:, qc + HD :]
    gain.finish()
    gain_sum[...] = jnp.sum(n_in[...], axis=0)
    wide = lambda ref, i: ref[i].astype(F32)
    for tree in (out, gn, go):
        tree.finish()
    out_sum[...] = (wide(b3, 0) + wide(b3, 1)) + (wide(b3, 2) + wide(b3, 3))
    go_sum[...] = (wide(c3, 0) + wide(c3, 1)) + (wide(c3, 2) + wide(c3, 3))
    for m in range(2):
        gn_sum[m] = wide(a3, 2 * m) + wide(a3, 2 * m + 1)


def finish_call(gn, out, go, gu, qkv, gain, ff, kw):
    dps = lax.axis_size("dp")
    any_ = pl.BlockSpec(memory_space=pl.ANY)
    vm = pl.BlockSpec(memory_space=pltpu.VMEM)
    dma = pltpu.SemaphoreType.DMA
    sds = jax.ShapeDtypeStruct
    scratch, sems = [], []
    for a in (gn, out, go):
        r, w = a.shape[-2:]
        scratch += [pltpu.VMEM((4, 2, r, w), BF), pltpu.VMEM((4, 2, r, w), BF),
                    pltpu.VMEM((4, r, w), BF), pltpu.VMEM((4, r, w), BF)]
        sems += [dma((4, 2)), dma((4, 2)), dma((4,)), dma((4,)), dma((4, 2)), dma((4,)), dma((4,))]
    wrows, width = go.shape[-2:]
    wide = pltpu.VMEM((dps, 2, 4, wrows, width), BF)
    qb, nb = qkv.shape[1:], gain.shape[1:]
    return pl.pallas_call(
        finish_kernel,
        out_shape=(
            sds((2,) + gn.shape[-2:], F32), sds(out.shape[-2:], F32), sds(go.shape[-2:], F32),
            sds((wrows, ff), F32), sds((wrows, ff), F32),
            sds((wrows, width), F32), sds((wrows, kw), F32), sds((wrows, kw), F32),
            sds(gain.shape[-2:], F32),
        ),
        in_specs=[any_] * 6,
        out_specs=(vm,) * 9,
        scratch_shapes=scratch + sems + [
            wide, wide, wide, dma((dps, 2)), dma((dps, 2)), dma((dps, 2)), dma((dps,)), dma((dps,)),
            pltpu.VMEM(gu.shape, BF), dma((16,)), dma((16,)),
            pltpu.VMEM(qb, BF), pltpu.VMEM((dps,) + qb, BF), pltpu.VMEM(qb, BF),
            dma((16,)), dma((16,)), dma((dps,)), dma((dps,)), dma((1,)),
            pltpu.VMEM(nb, F32), pltpu.VMEM((dps,) + nb, F32), pltpu.VMEM(nb, F32),
            dma((16,)), dma((16,)), dma((dps,)), dma((dps,)), dma((1,)),
        ],
        compiler_params=pltpu.CompilerParams(collective_id=2, has_side_effects=True, vmem_limit_bytes=56 << 20),
        name="finish",
    )(gn, out, go, gu, qkv, gain)


def sum_over_groups(a):
    dps = lax.axis_size("dp")
    d = lax.axis_index("dp")
    total = lax.dynamic_index_in_dim(a, d, 0, keepdims=False).astype(F32)
    for r in range(1, dps):
        there = lax.dynamic_index_in_dim(a, (d + r) % dps, 0, keepdims=False)
        total = total + lax.ppermute(there, "dp", [(i, (i + r) % dps) for i in range(dps)]).astype(F32)
    return total


def swap_halves(a):
    h = a.shape[-1] // 2
    return jnp.concatenate([a[:, h:], a[:, :h]], axis=-1)


BLOCK = 256


def attention_kernel(x_ref, qkv_ref, pre_ref, hg_ref, cos_ref, sin_ref, docc_ref, docr_ref, plc_ref, plr_ref,
                     normed_ref, raw_ref, q_ref, k_ref, v_ref, att_ref, lse_ref, mixed_ref):
    length = x_ref.shape[0]
    group = q_ref.shape[0]
    steps = length // BLOCK

    def project(i, carry):
        at = pl.ds(pl.multiple_of(i * BLOCK, BLOCK), BLOCK)
        x = x_ref[at, :].astype(F32)
        normed = rms_norm(x, pre_ref[...]).astype(BF)
        normed_ref[at, :] = normed
        raw = dot(normed, qkv_ref[...])
        raw_ref[at, :] = raw
        c, s = cos_ref[at, :], sin_ref[at, :]
        for h in range(group + 1):
            n = rms_norm(raw[:, h * HD : (h + 1) * HD], hg_ref[0 if h < group else 1][None, :])
            n = (n * c + swap_halves(n) * s).astype(BF)
            if h < group:
                q_ref[h, at, :] = n
            else:
                k_ref[at, :] = n
        v_ref[at, :] = raw[:, (group + 1) * HD :].astype(BF)
        return carry

    lax.fori_loop(0, steps, project, 0)

    def attend(i, carry):
        at = pl.ds(pl.multiple_of(i * BLOCK, BLOCK), BLOCK)
        allowed = (docc_ref[at, :] == docr_ref[...]) & (plr_ref[...] <= plc_ref[at, :])
        bias = jnp.where(allowed, 0.0, -1e30)
        for h in range(group):
            scores = dot_nt(q_ref[h, at, :] * HD**-0.5, k_ref[...]) + bias
            top = jnp.max(scores, axis=-1, keepdims=True)
            p = jnp.exp(scores - top)
            total = jnp.sum(p, axis=-1, keepdims=True)
            out = dot(p.astype(BF), v_ref[...]) / total
            att_ref[h, at, :] = out
            lse_ref[h, at, :] = top + jnp.log(total)
            mixed_ref[at, h * HD : (h + 1) * HD] = out.astype(BF)
        return carry

    lax.fori_loop(0, steps, attend, 0)


def attention_call(x, qkv, pre, hg, cos, sin, doc, place):
    length, width = x.shape
    cols = qkv.shape[1]
    group = cols // HD - 2
    vm = pl.BlockSpec(memory_space=pltpu.VMEM)
    sds = jax.ShapeDtypeStruct
    return pl.pallas_call(
        attention_kernel,
        out_shape=(
            sds((length, width), BF), sds((length, cols), F32), sds((group, length, HD), BF),
            sds((length, HD), BF), sds((length, HD), BF), sds((group, length, HD), F32),
            sds((group, length, 1), F32), sds((length, group * HD), BF),
        ),
        in_specs=[vm] * 10,
        out_specs=(vm,) * 8,
        compiler_params=pltpu.CompilerParams(vmem_limit_bytes=50 << 20),
        name="attention",
    )(x, qkv, pre.reshape(1, -1), hg, cos, sin, doc[:, None], doc[None, :], place[:, None], place[None, :])


def attention_back_kernel(gm_ref, att_ref, lse_ref, q_ref, k_ref, v_ref, raw_ref, normed_ref, x_ref, qkv_ref,
                          hg_ref, cos_ref, sin_ref, docc_ref, docr_ref, plc_ref, plr_ref,
                          gqkv_ref, gn_ref, gpre_ref, ghead_ref, dk, dv, dq, low):
    length = x_ref.shape[0]
    group = q_ref.shape[0]
    steps = length // BLOCK
    dk[...] = jnp.zeros_like(dk)
    dv[...] = jnp.zeros_like(dv)

    def attend(i, carry):
        at = pl.ds(pl.multiple_of(i * BLOCK, BLOCK), BLOCK)
        allowed = (docc_ref[at, :] == docr_ref[...]) & (plr_ref[...] <= plc_ref[at, :])
        bias = jnp.where(allowed, 0.0, -1e30)
        for h in range(group):
            q = q_ref[h, at, :]
            gm = gm_ref[at, h * HD : (h + 1) * HD]
            delta = jnp.sum(gm.astype(F32) * att_ref[h, at, :], axis=-1, keepdims=True)
            p = jnp.exp(dot_nt(q * HD**-0.5, k_ref[...]) + bias - lse_ref[h, at, :])
            dv[...] += dot_tn(p.astype(BF), gm)
            gs = (p * (dot_nt(gm, v_ref[...]) - delta)).astype(BF)
            dq[h, at, :] = dot(gs, k_ref[...]) * HD**-0.5
            dk[...] += dot_tn(gs, q)
        return carry

    lax.fori_loop(0, steps, attend, 0)

    def back(i, carry):
        g_pre, g_q, g_k = carry
        at = pl.ds(pl.multiple_of(i * BLOCK, BLOCK), BLOCK)
        c, s = cos_ref[at, :], sin_ref[at, :]
        for h in range(group + 1):
            u = raw_ref[at, h * HD : (h + 1) * HD]
            gain = hg_ref[0 if h < group else 1][None, :]
            dy = dq[h, at, :] if h < group else dk[at, :] * HD**-0.5
            dn = dy * c - swap_halves(dy) * s
            r = lax.rsqrt(jnp.mean(u * u, axis=-1, keepdims=True) + EPS)
            dgain = jnp.sum(dn * u * r, axis=0, keepdims=True)
            t = gain * dn
            du = r * t - u * (r * r * r) * jnp.mean(u * t, axis=-1, keepdims=True)
            low[at, h * HD : (h + 1) * HD] = du.astype(BF)
            if h < group:
                g_q = g_q + dgain
            else:
                g_k = g_k + dgain
        low[at, (group + 1) * HD :] = dv[at, :].astype(BF)
        part = dot_nt(low[at, :], qkv_ref[...])
        gn_ref[at, :] = part.astype(BF)
        x = x_ref[at, :].astype(F32)
        r = lax.rsqrt(jnp.mean(x * x, axis=-1, keepdims=True) + EPS)
        g_pre = g_pre + jnp.sum(part * (x * r), axis=0, keepdims=True)
        return g_pre, g_q, g_k

    zero = jnp.zeros((1, HD), F32)
    g_pre, g_q, g_k = lax.fori_loop(0, steps, back, (jnp.zeros((1, x_ref.shape[1]), F32), zero, zero))
    gpre_ref[...] = g_pre
    ghead_ref[0:1, :] = g_q
    ghead_ref[1:2, :] = g_k
    gqkv_ref[...] = dot_tn(normed_ref[...], low[...]).astype(BF)


def attention_back_call(gm, att, lse, q, k, v, raw, normed, x, qkv, hg, cos, sin, doc, place):
    length, width = x.shape
    cols = qkv.shape[1]
    group = q.shape[0]
    vm = pl.BlockSpec(memory_space=pltpu.VMEM)
    sds = jax.ShapeDtypeStruct
    return pl.pallas_call(
        attention_back_kernel,
        out_shape=(sds((width, cols), BF), sds((length, width), BF), sds((1, width), F32), sds((2, HD), F32)),
        in_specs=[vm] * 17,
        out_specs=(vm,) * 4,
        scratch_shapes=[
            pltpu.VMEM((length, HD), F32), pltpu.VMEM((length, HD), F32),
            pltpu.VMEM((group, length, HD), F32), pltpu.VMEM((length, cols), BF),
        ],
        compiler_params=pltpu.CompilerParams(vmem_limit_bytes=50 << 20),
        name="attention_back",
    )(gm, att, lse, q, k, v, raw, normed, x, qkv, hg, cos, sin,
      doc[:, None], doc[None, :], place[:, None], place[None, :])


def local(tokens, cotangent, segments, span_order, pre_gain, query_proj, key_proj, value_proj,
          head_gain, out_proj, mid_gain, gate_proj, up_proj, down_proj):
    micros, seqs, rows, width = tokens.shape
    both = ("dp", "cp")
    cp = lax.axis_size("cp")
    dp = lax.axis_size("dp")
    me = lax.axis_index("cp")
    length = rows * cp
    kvh = key_proj.shape[1] // HD
    group = query_proj.shape[1] // key_proj.shape[1]
    qcols = group * HD
    wrows = gate_proj.shape[0]
    ffs = down_proj.shape[0]
    own = micros * seqs * rows
    my_seq, my_head = me // kvh, me % kvh

    half = dp * ffs
    padded = -(-half // 128) * 128
    packed = jnp.concatenate([pre_gain, mid_gain, head_gain]).astype(F32)
    packed = jnp.pad(packed, (0, 128 - packed.shape[0])).reshape(1, 128)
    packed = jnp.broadcast_to(packed, (8, 128))
    x_own = tokens.reshape(own, width)
    cot_own = cotangent.reshape(own, width)
    x_seq, c_all, qkv, gu_w, down_w, gains = start_call(
        tokens.reshape(micros, rows, width), cot_own, query_proj, key_proj, value_proj, gate_proj, up_proj,
        down_proj, packed
    )
    qkv = qkv.reshape(dp * cp * wrows, -1)
    gu_w = gu_w.reshape(dp * cp * wrows, -1)
    down_w = down_w.reshape(half, width)
    gains = gains.reshape(dp * cp, 8, 128)[:, 0]
    pre_full = gains[:, :wrows].reshape(-1)
    mid_full = gains[:, wrows : 2 * wrows].reshape(-1)
    head_full = gains[:, 2 * wrows : 2 * wrows + head_gain.shape[0]].reshape(-1)
    out_full = lax.all_gather(out_proj, both, axis=0, tiled=True)

    spans = span_order.shape[0]
    span_rows = length // spans
    places = (span_order[:, None] * span_rows + jnp.arange(span_rows, dtype=jnp.int32)[None, :]).reshape(length)
    docs_seq = lax.dynamic_index_in_dim(segments.reshape(-1, length), my_seq, 0, keepdims=False)
    chosen = (span_order[:, None] == jnp.arange(spans, dtype=jnp.int32)[None, :]).astype(jnp.int32)
    docs = jnp.sum(chosen[:, :, None] * docs_seq.reshape(1, spans, span_rows), axis=1).reshape(length)
    firsts = jnp.sum((docs_seq[None, :] < docs[:, None]).astype(jnp.int32), axis=1)
    frequency = THETA ** (-jnp.arange(0, HD, 2).astype(F32) / HD)
    angles = (places - firsts).astype(F32)[:, None] * frequency
    cos, sin = jnp.cos(angles), jnp.sin(angles)
    cos = jnp.concatenate([cos, cos], axis=-1)
    sin = jnp.concatenate([-sin, sin], axis=-1)

    x_seq = x_seq.reshape(length, width)
    head_gains = head_full.reshape(2, HD)
    normed, raw, q, k, v, attended, log_total, mixed_mine = attention_call(
        x_seq, qkv, pre_full, head_gains, cos, sin, docs, places
    )

    def to_tokens(a):
        a = lax.all_to_all(a.reshape(cp, rows, qcols), "cp", 0, 0, tiled=True)
        return a.reshape(micros * seqs, kvh, rows, qcols).transpose(0, 2, 1, 3).reshape(own, kvh * qcols)

    def to_heads(a):
        a = a.reshape(micros * seqs, rows, kvh, qcols).transpose(0, 2, 1, 3).reshape(cp, rows, qcols)
        return lax.all_to_all(a, "cp", 0, 0, tiled=True).reshape(length, qcols)

    mixed = to_tokens(mixed_mine)
    middle = x_own.astype(F32) + dot(mixed, out_full)
    normed_mid = rms_norm(middle, mid_full).astype(BF)

    gnm, out_part, g_gu, g_down = ffn_call(normed_mid, c_all, gu_w, down_w)
    g_down = sum_over_groups(g_down[:half].reshape(dp, ffs, width))
    g_gu = sum_over_groups(g_gu.reshape(dp, cp, wrows, -1)).astype(BF)

    unused, mid_pull = jax.vjp(rms_norm, middle, mid_full)
    part, g_mid = mid_pull(gnm)
    grad_middle = cot_own.astype(F32) + part
    branch = grad_middle.astype(BF)
    g_out = dot_tn(mixed, branch).astype(BF)
    g_out = g_out.reshape(dp, 4, 2, 2, wrows, width).transpose(0, 2, 3, 1, 4, 5)
    grad_mixed = to_heads(dot_nt(branch, out_full).astype(BF))
    g_qkv, gn_part, g_pre, g_head = attention_back_call(
        grad_mixed, attended, log_total, q, k, v, raw, normed, x_seq, qkv, head_gains, cos, sin, docs, places
    )
    g_qkv = g_qkv.reshape(dp, cp, wrows, -1)
    small = jnp.concatenate([
        g_pre.reshape(dp * cp, -1), g_mid.reshape(dp * cp, -1),
        g_head.reshape(dp * cp, -1)], axis=-1)
    small = jnp.pad(small, ((0, 0), (0, 128 - small.shape[1]))).reshape(dp, cp, 1, 128)
    small = jnp.broadcast_to(small, (dp, cp, 8, 128))
    gn, out_rows, g_out, g_gate_own, g_up_own, g_query, g_key, g_value, small = finish_call(
        gn_part.reshape(4, 2, 2, rows, width), out_part, g_out, g_gu, g_qkv, small, gate_proj.shape[1], key_proj.shape[1]
    )
    block_out = (middle + out_rows).astype(BF)
    x32 = x_own.astype(F32)
    r_own = lax.rsqrt(jnp.mean(x32 * x32, axis=-1, keepdims=True) + EPS)
    g_dn = gn.reshape(own, width) * pre_full
    grad_tokens = grad_middle + r_own * g_dn - x32 * r_own**3 * jnp.mean(x32 * g_dn, axis=-1, keepdims=True)
    small = small[0]
    g_head = small[2 * wrows : 2 * wrows + head_gain.shape[0]]
    return (
        block_out.reshape(tokens.shape), grad_tokens.reshape(tokens.shape),
        small[:wrows], g_query, g_key, g_value, g_head, g_out,
        small[wrows : 2 * wrows], g_gate_own, g_up_own, g_down,
    )


def solution(mesh):
    both = ("dp", "cp")
    act = P(None, "dp", "cp", None)
    mat, vec = P(both, None), P(both)
    return jax.shard_map(
        local,
        mesh=mesh,
        in_specs=(act, act, P(None, "dp", None), P(), vec, mat, mat, mat, vec, mat, vec, mat, mat, mat),
        out_specs=(act, act, vec, mat, mat, mat, vec, mat, vec, mat, mat, mat),
        check_vma=False,
    )
```
